32 devices in a mesh: groups: 2 (over y), tile: 16 (over z, x, core).
Axes of the slice: x: 2, y: 2, z: 4, core: 2. Of those that a mesh axis runs over, the one named last changes fastest.
Arguments:
- features: bfloat16 [64, 12288], P(None, ('groups', 'tile')), parts along dimension 1, may hold values from -6 to 6
- rulebook: int32 [27, 12288], P(None, ('groups', 'tile')), parts along dimension 1, may hold values from 0 to 640, as said below
- send_lists: int32 [2, 32], P(None, ('groups', 'tile')), parts along dimension 1, may hold values from 0 to 3, as said below
- weight_first: bfloat16 [64, 1728], replicated, may hold values from -0.375 to 0.375
- weight_second: bfloat16 [64, 1728], replicated, may hold values from -0.75 to 0.75
- cotangent: bfloat16 [64, 12288], P(None, ('groups', 'tile')), parts along dimension 1, may hold values from -6 to 6
Outputs:
- out_features: bfloat16 [64, 12288], P(None, ('groups', 'tile')), parts along dimension 1
- d_features: bfloat16 [64, 12288], P(None, ('groups', 'tile')), parts along dimension 1
- grad_first: float32 [128, 1728], P('groups'), parts along dimension 0
- grad_second: float32 [128, 1728], P('groups'), parts along dimension 0
The draws below stay inside these ranges and needn't reach their ends.
There are 2 independent parts, one for each index of `groups`. The reference program is written for one: setup_inputs(seed, part) draws one part's arguments, and reference() takes and returns one part's arrays. A program takes and returns all parts, laid end to end along the dimension named above; an argument that names none is the same for every part. Nothing has to cross between parts.
Inputs may be any that keep to these rules, and one draw needn't show every extreme that they name: `rulebook`: A tile's rows are occupied cells of its box of 3 x 64 x 16 lattice cells, exactly 128 of them in each plane; tile t borders tile t - 1 below and t + 1 above along the first dimension. Offset k = 9 (a + 1) + 3 (b + 1) + (c + 1), with a, b, c in -1, 0, 1, names the occupied cell at that displacement, or 640 where that cell is empty or outside the detector; offset 27 // 2 names the row itself. If offset k of voxel v names voxel u, then offset 27 - 1 - k of u names v. Every halo row that is named lies in a listed block. `send_lists`: row 0 of a tile lists the distinct blocks of it that hold the cells of its lowest plane, row 1 those that hold the cells of its highest plane, 1 block each; the first tile lists nothing in row 0 and the last nothing in row 1, their entries being 3.
All inputs are finite; a program needn't handle non-finite values.
Results may differ from the reference program's by a relative error of at most 0.0042.
Values may be sent and summed in bfloat16 or wider, within the bound.
A program may use at most 64 MiB of HBM per device.

```python
import math
import jax
import jax.numpy as jnp
from jax import lax

CHANNELS = 64
OFFSETS = 27
PLANES = 3
SIDE_Z = 16
PLANE_BLOCKS = 1
SIDE_Y = 64
VOX_DEV = 384
BLOCKS_DEV = 3
HALO_ROWS = 128
VOXELS = 6144
N_TILE = 16


def geometry(key):
    plane = SIDE_Y * SIDE_Z
    cells = PLANES * plane
    per_plane = PLANE_BLOCKS * 128
    missing = VOX_DEV + 2 * HALO_ROWS
    base = jax.random.fold_in(key, 4242)
    score_key, order_key = jax.random.split(base)
    plane_ids = jnp.arange(plane, dtype=jnp.int32)
    tiles = jnp.arange(N_TILE, dtype=jnp.int32)
    scores = jax.random.randint(score_key, (N_TILE, PLANES, plane), 0, 1 << 16, dtype=jnp.int32) * plane + plane_ids[None, None, :]
    picked = jnp.argsort(scores, axis=2, stable=True)[:, :, :per_plane].astype(jnp.int32)
    picked = jnp.sort(picked, axis=2) + (jnp.arange(PLANES, dtype=jnp.int32) * plane)[None, :, None]
    chosen = picked.reshape(N_TILE, VOX_DEV).astype(jnp.int32)
    perms = jax.vmap(lambda subkey: jax.random.permutation(subkey, BLOCKS_DEV).astype(jnp.int32))(jax.random.split(order_key, N_TILE))
    inverse = jnp.argsort(perms, axis=1, stable=True).astype(jnp.int32)
    positions = jnp.arange(VOX_DEV, dtype=jnp.int32)
    old_positions = jnp.full((N_TILE, cells), -1, jnp.int32).at[tiles[:, None], chosen].set(jnp.broadcast_to(positions[None, :], (N_TILE, VOX_DEV)))
    lowest = jnp.sum((chosen < plane).astype(jnp.int32), axis=1)
    highest = jnp.sum((chosen >= cells - plane).astype(jnp.int32), axis=1)
    low_count = jnp.where(tiles == 0, 0, (lowest + 127) // 128)
    high_count = jnp.where(tiles == N_TILE - 1, 0, (highest + 127) // 128)
    slots = jnp.arange(PLANE_BLOCKS, dtype=jnp.int32)[None, :]
    down_list = jnp.where(slots < low_count[:, None], inverse[:, :PLANE_BLOCKS], BLOCKS_DEV)
    up_old = jnp.clip(BLOCKS_DEV - high_count[:, None] + slots, 0, BLOCKS_DEV - 1)
    up_list = jnp.where(slots < high_count[:, None], jnp.take_along_axis(inverse, up_old, axis=1), BLOCKS_DEV)
    lists = jnp.stack([down_list, up_list]).reshape(2, N_TILE * PLANE_BLOCKS).astype(jnp.int32)
    rows = jnp.arange(VOX_DEV, dtype=jnp.int32)
    old_of_row = perms[:, rows // 128] * 128 + (rows % 128)[None, :]
    cell = jnp.take_along_axis(chosen, old_of_row, axis=1)
    coord_x = cell // plane
    coord_y = cell % plane // SIDE_Z
    coord_z = cell % SIDE_Z
    offsets = jnp.arange(OFFSETS, dtype=jnp.int32)[:, None, None]
    near_x = coord_x[None] + offsets // 9 - 1
    near_y = coord_y[None] + offsets // 3 % 3 - 1
    near_z = coord_z[None] + offsets % 3 - 1
    inside = (near_y >= 0) & (near_y < SIDE_Y) & (near_z >= 0) & (near_z < SIDE_Z)
    across = jnp.clip(near_y, 0, SIDE_Y - 1) * SIDE_Z + jnp.clip(near_z, 0, SIDE_Z - 1)
    owner = tiles[None, :, None]
    here = old_positions[owner, jnp.clip(near_x, 0, PLANES - 1) * plane + across]
    here_safe = jnp.maximum(here, 0)
    here_rule = inverse[owner, here_safe // 128] * 128 + here_safe % 128
    below_tile = jnp.clip(owner - 1, 0, N_TILE - 1)
    below = old_positions[below_tile, (PLANES - 1) * plane + across]
    below_safe = jnp.maximum(below, 0)
    below_rule = VOX_DEV + (below_safe // 128 - (BLOCKS_DEV - high_count[below_tile])) * 128 + below_safe % 128
    above_tile = jnp.clip(owner + 1, 0, N_TILE - 1)
    above = old_positions[above_tile, across]
    above_rule = VOX_DEV + HALO_ROWS + jnp.maximum(above, 0)
    rule = jnp.where((near_x >= 0) & (near_x < PLANES) & (here >= 0), here_rule, missing)
    rule = jnp.where((near_x < 0) & (owner > 0) & (below >= 0), below_rule, rule)
    rule = jnp.where((near_x >= PLANES) & (owner < N_TILE - 1) & (above >= 0), above_rule, rule)
    rule = jnp.where(inside, rule, missing)
    return (rule.reshape(OFFSETS, N_TILE * VOX_DEV).astype(jnp.int32), lists)


def draw_rulebook(key, part):
    return geometry(key)[0]


def draw_send_lists(key, part):
    return geometry(key)[1]


def level_of(stream_key, extent, cuts, low, high):
    loudness, own = 1.0, jax.random.fold_in(stream_key, 6)
    for axis_at, blocks in cuts:
        heights = jnp.exp(jax.random.uniform(jax.random.fold_in(own, axis_at), (blocks,), jnp.float32, low / len(cuts), high / len(cuts)))
        loudness = loudness * jnp.repeat(heights, extent[axis_at] // blocks).reshape([-1 if axis == axis_at else 1 for axis in range(len(extent))])
    return loudness


def bell_draw(rng, dims, scale, most, cuts=(), kind=jnp.bfloat16):
    entries = jax.random.normal(rng, dims, jnp.float32) * scale
    if len(cuts) > 0:
        entries = level_of(rng, dims, cuts, -0.22, 0.18) * entries
    return jnp.clip(entries, min=-most, max=most).astype(kind)


def setup_inputs(seed: int = 0, part: int = 0) -> dict:
    splits = jax.random.split(jax.random.key(seed), 7)
    part_splits = jax.random.split(jax.random.fold_in(splits[6], part), 7)
    return {
        "features": bell_draw(part_splits[0], (CHANNELS, VOXELS), 1.0, 6.0, ((1, 16),)),
        "rulebook": draw_rulebook(jax.random.fold_in(jax.random.fold_in(splits[6], part), 71), part),
        "send_lists": draw_send_lists(jax.random.fold_in(jax.random.fold_in(splits[6], part), 71), part),
        "weight_first": bell_draw(splits[3], (CHANNELS, OFFSETS * CHANNELS), (OFFSETS * CHANNELS // 6) ** -0.5, 0.375),
        "weight_second": bell_draw(splits[4], (CHANNELS, OFFSETS * CHANNELS), (OFFSETS * CHANNELS // 24) ** -0.5, 0.75),
        "cotangent": bell_draw(part_splits[5], (CHANNELS, VOXELS), 1.0, 6.0, ((1, 16),)),
    }


def global_index(rulebook, send_lists):
    ids = rulebook.reshape(OFFSETS, N_TILE, VOX_DEV)
    lists = send_lists.reshape(2, N_TILE, PLANE_BLOCKS)
    tiles = jnp.arange(N_TILE, dtype=jnp.int32)[None, :, None]
    below_tile = jnp.clip(tiles - 1, 0, N_TILE - 1)
    above_tile = jnp.clip(tiles + 1, 0, N_TILE - 1)
    low_offset = jnp.clip(ids - VOX_DEV, 0, HALO_ROWS - 1)
    high_offset = jnp.clip(ids - VOX_DEV - HALO_ROWS, 0, HALO_ROWS - 1)
    below_block = lists[1][below_tile, low_offset // 128]
    above_block = lists[0][above_tile, high_offset // 128]
    below_row = below_tile * VOX_DEV + below_block * 128 + low_offset % 128
    above_row = above_tile * VOX_DEV + above_block * 128 + high_offset % 128
    result = jnp.full(ids.shape, VOXELS, jnp.int32)
    result = jnp.where(ids < VOX_DEV, tiles * VOX_DEV + ids, result)
    lower_ok = (ids >= VOX_DEV) & (ids < VOX_DEV + HALO_ROWS) & (tiles > 0) & (below_block < BLOCKS_DEV)
    upper_ok = (ids >= VOX_DEV + HALO_ROWS) & (ids < VOX_DEV + 2 * HALO_ROWS) & (tiles < N_TILE - 1) & (above_block < BLOCKS_DEV)
    result = jnp.where(lower_ok, below_row, result)
    result = jnp.where(upper_ok, above_row, result)
    return result.transpose(1, 0, 2).astype(jnp.int32)

def padded_of(values):
    return jnp.concatenate([values, jnp.zeros((values.shape[0], 1), values.dtype)], axis=1)

def columns_of(padded, indices):
    gathered = padded[:, indices]
    return gathered.transpose(1, 0, 2).reshape(-1, indices.shape[1])

def convolve(weight, values, index):
    padded = padded_of(values)
    result = lax.map(lambda indices: jnp.dot(weight, columns_of(padded, indices), preferred_element_type=jnp.float32), index)
    return result.transpose(1, 0, 2).reshape(values.shape[0], -1)

def weight_grad(grads, values, index):
    width = grads.shape[0]
    padded = padded_of(values)
    pieces = grads.reshape(width, N_TILE, VOX_DEV).transpose(1, 0, 2)

    def step(total, pair):
        piece, indices = pair
        term = lax.dot_general(piece, columns_of(padded, indices), (((1,), (1,)), ((), ())), preferred_element_type=jnp.float32)
        return (total + term, None)
    total, unused = lax.scan(step, jnp.zeros((width, OFFSETS * width), jnp.float32), (pieces, index))
    return total

def spread_back(weight, grads, index):
    width = grads.shape[0]
    pieces = grads.reshape(width, N_TILE, VOX_DEV).transpose(1, 0, 2)

    def step(total, pair):
        piece, indices = pair
        terms = jnp.dot(weight.T, piece, preferred_element_type=jnp.float32)
        terms = terms.reshape(OFFSETS, width, -1).transpose(1, 0, 2)
        return (total.at[:, indices].add(terms), None)
    total, unused = lax.scan(step, jnp.zeros((width, VOXELS + 1), jnp.float32), (pieces, index))
    return total[:, :VOXELS]

def reference(features, rulebook, send_lists, weight_first, weight_second, cotangent):
    index = global_index(rulebook, send_lists)
    pre_first = convolve(weight_first, features, index)
    hidden = jax.nn.silu(pre_first).astype(jnp.bfloat16)
    out_features = (convolve(weight_second, hidden, index) + features.astype(jnp.float32)).astype(jnp.bfloat16)
    scale = 1.0 / math.sqrt(VOXELS)
    grad_second = weight_grad(cotangent, hidden, index) * scale
    d_hidden = spread_back(weight_second, cotangent, index)
    sigma = jax.nn.sigmoid(pre_first)
    d_pre = (d_hidden * sigma * (1.0 + pre_first * (1.0 - sigma))).astype(jnp.bfloat16)
    grad_first = weight_grad(d_pre, features, index) * scale
    d_features = (cotangent.astype(jnp.float32) + spread_back(weight_first, d_pre, index)).astype(jnp.bfloat16)
    return (out_features, d_features, grad_first, grad_second)
```

```python
import functools
import math

import jax
import jax.numpy as jnp
from jax import lax
from jax.experimental import pallas as pl
from jax.experimental.pallas import tpu as pltpu
from jax.sharding import PartitionSpec as P

LANES = 128
BF = jnp.bfloat16
F32 = jnp.float32
TRANS_RHS = (((1,), (1,)), ((), ()))


def chunk_plan(width, cols, chips):
    row_parts = math.gcd(width // 16, chips)
    col_parts = chips // row_parts
    piece_cols = -(-cols // (col_parts * LANES)) * LANES
    return row_parts, col_parts, width // row_parts, piece_cols


def kernel(
    count, plan, scale,
    x_ref, rule_ref, lists_ref, w1_ref, w2_ref, cot_ref,
    out_ref, dx_ref, g1_ref, g2_ref,
    hot, gat_a, gat_b, mir1, mir2, own, hsend, halo, part, peer_in, rs_out, rs_in, ag,
    hs_sem, hr_sem, p_sem, rs_s, rs_r, ag_s, ag_r, fw_s, fw_r,
):
    width, rows = x_ref.shape
    offsets = rule_ref.shape[0]
    group = offsets // 3
    blocks = rows // LANES
    chips = count // 2
    row_parts, col_parts, piece_rows, piece_cols = plan
    missing = rows + 2 * LANES
    t = lax.axis_index("tile")
    core = lax.rem(t, 2)
    chip = t // 2
    peer = t + 1 - 2 * core

    def lanes(b):
        return slice(b * LANES, (b + 1) * LANES)

    def there(distance):
        return 2 * lax.rem(chip + distance, chips) + core

    barrier = pltpu.get_barrier_semaphore()
    beside = lax.rem(t + 2 * core - 1 + count, count)
    pl.semaphore_signal(barrier, inc=1, device_id={"tile": peer})
    pl.semaphore_signal(barrier, inc=1, device_id={"tile": beside})
    for d in range(1, chips):
        pl.semaphore_signal(barrier, inc=1, device_id={"tile": there(d)})

    def halo_copy(phase, up):
        return pltpu.make_async_remote_copy(
            src_ref=hsend.at[phase, up],
            dst_ref=halo.at[phase, 1 - up],
            send_sem=hs_sem.at[phase, up],
            recv_sem=hr_sem.at[phase, 1 - up],
            device_id={"tile": t + 2 * up - 1},
        )

    def pick_boundary(phase):
        for up in range(2):
            listed = jnp.broadcast_to(lists_ref[up : up + 1, :], (2 * width, LANES))
            chosen = jnp.zeros((2 * width, LANES), F32)
            for q in range(blocks):
                chosen = jnp.where(listed == q, own[phase, q], chosen)
            hsend[phase, up] = chosen.astype(BF)

    def send_halo(phase):
        @pl.when(t > 0)
        def _():
            halo_copy(phase, 0).start()

        @pl.when(t < count - 1)
        def _():
            halo_copy(phase, 1).start()

    def wait_halo(phase):
        @pl.when(t > 0)
        def _():
            halo_copy(phase, 1).wait_recv()

        @pl.when(t == 0)
        def _():
            halo[phase, 0] = jnp.zeros((2 * width, LANES), BF)

        @pl.when(t < count - 1)
        def _():
            halo_copy(phase, 0).wait_recv()

        @pl.when(t == count - 1)
        def _():
            halo[phase, 1] = jnp.zeros((2 * width, LANES), BF)

    def wait_sent(phase):
        @pl.when(t > 0)
        def _():
            halo_copy(phase, 0).wait_send()

        @pl.when(t < count - 1)
        def _():
            halo_copy(phase, 1).wait_send()

    for q in range(blocks):
        own[0, q] = jnp.concatenate([x_ref[:, lanes(q)], cot_ref[:, lanes(q)]], axis=0).astype(F32)
    pick_boundary(0)
    pl.semaphore_wait(barrier, chips + 1)
    send_halo(0)

    reach = jax.lax.broadcasted_iota(jnp.int32, (LANES, LANES), 0)
    firsts = {}
    for a in range(3):
        for b in range(blocks):
            base = b * LANES
            if a != 1:
                low = rule_ref[a * group : a * group + 1, lanes(b)]
                for j in range(1, group):
                    k = a * group + j
                    low = jnp.minimum(low, rule_ref[k : k + 1, lanes(b)])
                low = jnp.min(low, axis=1, keepdims=True)
                firsts[a, b] = low
                base = jnp.zeros_like(low)
                for q in range(1, blocks + 2):
                    base = jnp.where((low >= q * LANES) & (low < missing), q * LANES, base)
            for j in range(group):
                k = a * group + j
                row = rule_ref[k : k + 1, lanes(b)] - base
                hit = jnp.broadcast_to(row, (LANES, LANES)) == reach
                hot[a, b, :, lanes(j)] = jnp.where(hit, 1.0, 0.0).astype(BF)

    for w_ref, m_ref in ((w2_ref, mir2), (w1_ref, mir1)):
        for k in range(0, offsets, 2):
            last = min(k + 2, offsets)
            stack = [
                w_ref[:, (offsets - 1 - i) * width : (offsets - i) * width].astype(F32)
                for i in range(k, last)
            ]
            stack = jnp.concatenate(stack, axis=0) if len(stack) > 1 else stack[0]
            m_ref[:, k * width : last * width] = stack.T.astype(BF)

    def gather(phase, a, b):
        if a == 1:
            source = own[phase, b]
        else:
            low = jnp.broadcast_to(firsts[a, b], (2 * width, LANES))
            source = None
            for q in range(blocks):
                if q != b:
                    block = own[phase, q]
                    if source is None:
                        source = block
                    else:
                        source = jnp.where((low >= q * LANES) & (low < (q + 1) * LANES), block, source)
            rim = halo[phase, a // 2].astype(F32)
            source = jnp.where((low >= rows) & (low < missing), rim, source)
        source = source.astype(BF)
        for j in range(0, group, 2):
            last = min(j + 2, group)
            res = jnp.dot(
                source, hot[a, b, :, j * LANES : last * LANES], preferred_element_type=F32
            ).astype(BF)
            for i in range(j, last):
                k = a * group + i
                gat_a[k * width : (k + 1) * width, lanes(b)] = res[:width, lanes(i - j)]
                gat_b[k * width : (k + 1) * width, lanes(b)] = res[width:, lanes(i - j)]

    for b in range(blocks):
        gather(0, 1, b)
    wait_halo(0)
    for a in (0, 2):
        for b in range(blocks):
            gather(0, a, b)

    pre = jnp.dot(w1_ref[...], gat_a[...], preferred_element_type=F32)
    d_hidden = jnp.dot(mir2[...], gat_b[...], preferred_element_type=F32)
    sigma = 1.0 / (1.0 + jnp.exp(-pre))
    hidden = (pre * sigma).astype(BF)
    d_pre = (d_hidden * sigma * (1.0 + pre * (1.0 - sigma))).astype(BF)
    both = jnp.concatenate([hidden, d_pre], axis=0).astype(F32)
    for q in range(blocks):
        own[1, q] = both[:, lanes(q)]
    pick_boundary(1)
    send_halo(1)

    cols = offsets * width
    to_peer = pltpu.make_async_remote_copy(
        src_ref=part.at[1 - core],
        dst_ref=peer_in,
        send_sem=p_sem.at[0],
        recv_sem=p_sem.at[1],
        device_id={"tile": peer},
    )
    spare = part.shape[2] - cols
    if spare:
        for g in range(2):
            part[g, :, cols:] = jnp.zeros((width, spare), F32)
    part[0, :, :cols] = lax.dot_general(d_pre, gat_a[...], TRANS_RHS, preferred_element_type=F32)

    @pl.when(core == 1)
    def _():
        to_peer.start()

    for k in range(0, offsets, 2):
        last = min(k + 2, offsets)
        top = (offsets - k) * width
        terms = lax.dot_general(
            gat_b[(offsets - last) * width : top, :], hidden, TRANS_RHS, preferred_element_type=F32
        )
        pieces = [
            terms[(last - 1 - i) * width : (last - i) * width, :] for i in range(k, last)
        ]
        pieces = jnp.concatenate(pieces, axis=1) if len(pieces) > 1 else pieces[0]
        part[1, :, k * width : last * width] = pieces

    @pl.when(core == 0)
    def _():
        to_peer.start()

    for b in range(blocks):
        gather(1, 1, b)

    def piece(j):
        r, c = (j // col_parts) * piece_rows, (j % col_parts) * piece_cols
        return slice(r, r + piece_rows), slice(c, c + piece_cols)

    to_peer.wait_recv()
    for j in range(chips):
        r, c = piece(j)
        rs_out[j] = (part[core, r, c] + peer_in[r, c]).astype(BF)

    def rs_copy(d):
        target = lax.rem(chip + d, chips)
        return pltpu.make_async_remote_copy(
            src_ref=rs_out.at[target],
            dst_ref=rs_in.at[chip],
            send_sem=rs_s.at[target],
            recv_sem=rs_r.at[chip],
            device_id={"tile": 2 * target + core},
        )

    def rs_arrival(d):
        source = lax.rem(chip + d, chips)
        return source, pltpu.make_async_remote_copy(
            src_ref=rs_out.at[source],
            dst_ref=rs_in.at[source],
            send_sem=rs_s.at[source],
            recv_sem=rs_r.at[source],
            device_id={"tile": 2 * source + core},
        )

    for d in range(1, chips):
        rs_copy(d).start()

    wait_halo(1)
    for a in (0, 2):
        for b in range(blocks):
            gather(1, a, b)
    second = jnp.dot(w2_ref[...], gat_a[...], preferred_element_type=F32)
    out_ref[...] = (second + x_ref[...].astype(F32)).astype(BF)
    d_input = jnp.dot(mir1[...], gat_b[...], preferred_element_type=F32)
    dx_ref[...] = (cot_ref[...].astype(F32) + d_input).astype(BF)

    total = rs_out[chip].astype(F32)
    for d in range(1, chips):
        source, arrival = rs_arrival(d)
        arrival.wait_recv()
        total = total + rs_in[source].astype(F32)
    ag[core, chip] = (total * scale).astype(BF)

    def ag_copy(d):
        target = lax.rem(chip + d, chips)
        return pltpu.make_async_remote_copy(
            src_ref=ag.at[core, chip],
            dst_ref=ag.at[core, chip],
            send_sem=ag_s.at[target],
            recv_sem=ag_r.at[chip],
            device_id={"tile": 2 * target + core},
        )

    def ag_arrival(source):
        return pltpu.make_async_remote_copy(
            src_ref=ag.at[core, source],
            dst_ref=ag.at[core, source],
            send_sem=ag_s.at[source],
            recv_sem=ag_r.at[source],
            device_id={"tile": 2 * source + core},
        )

    def forward(source):
        return pltpu.make_async_remote_copy(
            src_ref=ag.at[core, source],
            dst_ref=ag.at[core, source],
            send_sem=fw_s.at[source],
            recv_sem=fw_r.at[source],
            device_id={"tile": peer},
        )

    def forwarded(source):
        return pltpu.make_async_remote_copy(
            src_ref=ag.at[1 - core, source],
            dst_ref=ag.at[1 - core, source],
            send_sem=fw_s.at[source],
            recv_sem=fw_r.at[source],
            device_id={"tile": peer},
        )

    for d in range(1, chips):
        ag_copy(d).start()
    forward(chip).start()
    for d in range(1, chips):
        source = lax.rem(chip + chips - d, chips)
        ag_arrival(source).wait_recv()
        forward(source).start()
    for j in range(chips):
        forwarded(j).wait_recv()
    for j in range(chips):
        r, c = piece(j)
        live = min(c.stop, cols) - c.start
        if live > 0:
            place = slice(c.start, c.start + live)
            g1_ref[r, place] = ag[0, j, :, :live].astype(F32)
            g2_ref[r, place] = ag[1, j, :, :live].astype(F32)

    wait_sent(0)
    wait_sent(1)
    to_peer.wait_send()
    for d in range(1, chips):
        rs_copy(d).wait_send()
        ag_copy(d).wait_send()
    for j in range(chips):
        forward(j).wait_send()


def body(count, features, rulebook, send_lists, weight_first, weight_second, cotangent):
    width, rows = features.shape
    offsets = rulebook.shape[0]
    cols = offsets * width
    blocks = rows // LANES
    chips = count // 2
    plan = chunk_plan(width, cols, chips)
    row_parts, col_parts, piece_rows, piece_cols = plan
    scale = 1.0 / math.sqrt(rows * count)
    dma = pltpu.SemaphoreType.DMA
    vmem = pl.BlockSpec(memory_space=pltpu.VMEM)
    return pl.pallas_call(
        functools.partial(kernel, count, plan, scale),
        out_shape=(
            jax.ShapeDtypeStruct((width, rows), BF),
            jax.ShapeDtypeStruct((width, rows), BF),
            jax.ShapeDtypeStruct((width, cols), F32),
            jax.ShapeDtypeStruct((width, cols), F32),
        ),
        in_specs=[vmem] * 6,
        out_specs=(vmem,) * 4,
        scratch_shapes=[
            pltpu.VMEM((3, blocks, LANES, offsets // 3 * LANES), BF),
            pltpu.VMEM((cols, rows), BF),
            pltpu.VMEM((cols, rows), BF),
            pltpu.VMEM((width, cols), BF),
            pltpu.VMEM((width, cols), BF),
            pltpu.VMEM((2, blocks, 2 * width, LANES), F32),
            pltpu.VMEM((2, 2, 2 * width, LANES), BF),
            pltpu.VMEM((2, 2, 2 * width, LANES), BF),
            pltpu.VMEM((2, width, col_parts * piece_cols), F32),
            pltpu.VMEM((width, col_parts * piece_cols), F32),
            pltpu.VMEM((chips, piece_rows, piece_cols), BF),
            pltpu.VMEM((chips, piece_rows, piece_cols), BF),
            pltpu.VMEM((2, chips, piece_rows, piece_cols), BF),
            dma((2, 2)),
            dma((2, 2)),
            dma((2,)),
            dma((chips,)),
            dma((chips,)),
            dma((chips,)),
            dma((chips,)),
            dma((chips,)),
            dma((chips,)),
        ],
        compiler_params=pltpu.CompilerParams(
            collective_id=0, has_side_effects=True, vmem_limit_bytes=40 * 1024 * 1024
        ),
    )(features, rulebook, send_lists, weight_first, weight_second, cotangent)


def solution(mesh):
    split = P(None, ("groups", "tile"))
    return jax.shard_map(
        functools.partial(body, mesh.shape["tile"]),
        mesh=mesh,
        in_specs=(split, split, split, P(), P(), split),
        out_specs=(split, split, P("groups", None), P("groups", None)),
        check_vma=False,
    )
```

```python
import functools
import math

import jax
import jax.numpy as jnp
from jax import lax
from jax.experimental import pallas as pl
from jax.experimental.pallas import tpu as pltpu
from jax.sharding import PartitionSpec as P

LANES = 128
LIMIT_MIB = 60
BF = jnp.bfloat16
F32 = jnp.float32
TRANS_RHS = (((1,), (1,)), ((), ()))


def chunk_plan(width, cols, chips):
    row_parts = math.gcd(width // 16, chips)
    col_parts = chips // row_parts
    piece_cols = -(-cols // (col_parts * LANES)) * LANES
    return row_parts, col_parts, width // row_parts, piece_cols


def piece_of(plan, j):
    row_parts, col_parts, piece_rows, piece_cols = plan
    r, c = (j // col_parts) * piece_rows, (j % col_parts) * piece_cols
    return slice(r, r + piece_rows), slice(c, c + piece_cols)


def finish(plan, out_near, dx_near, ag_near, out_far, dx_far, g1_far, g2_far, ag, g_ref, sem):
    chips, cols = ag.shape[1], g_ref.shape[2]
    loads = [pltpu.make_async_copy(ag_near.at[g], ag.at[g], sem.at[g]) for g in range(2)]
    moves = [
        pltpu.make_async_copy(out_near, out_far, sem.at[2]),
        pltpu.make_async_copy(dx_near, dx_far, sem.at[3]),
        pltpu.make_async_copy(g_ref.at[0], g1_far, sem.at[4]),
        pltpu.make_async_copy(g_ref.at[1], g2_far, sem.at[5]),
    ]
    for copy in (loads[0], loads[1], moves[0], moves[1]):
        copy.start()
    for g in range(2):
        loads[g].wait()
        for j in range(chips):
            r, c = piece_of(plan, j)
            live = min(c.stop, cols) - c.start
            if live > 0:
                g_ref[g, r, c.start : c.start + live] = ag[g, j, :, :live].astype(F32)
        moves[2 + g].start()
    for copy in moves:
        copy.wait()


def kernel(
    count, plan, scale,
    x_hbm, rule_hbm, lists_hbm, w1_hbm, w2_hbm, cot_hbm,
    out_hbm, dx_hbm, ag,
    out_ref, dx_ref, mine, done_sem,
    x_ref, rule_ref, lists_ref, w1_ref, w2_ref, cot_ref, in_sem,
    hot, gat_a, gat_b, mir1, mir2, own, hsend, halo, part, peer_in, rs_out, rs_in,
    hs_sem, hr_sem, p_sem, rs_s, rs_r, ag_s, ag_r, fw_s, fw_r,
):
    width, rows = x_ref.shape
    offsets = rule_ref.shape[0]
    group = offsets // 3
    blocks = rows // LANES
    chips = count // 2
    row_parts, col_parts, piece_rows, piece_cols = plan
    missing = rows + 2 * LANES
    t = lax.axis_index("tile")
    core = lax.rem(t, 2)
    chip = t // 2
    peer = t + 1 - 2 * core

    def lanes(b):
        return slice(b * LANES, (b + 1) * LANES)

    def there(distance):
        return 2 * lax.rem(chip + distance, chips) + core

    x_in, cot_in, lists_in, rule_in, w1_in, w2_in = (
        pltpu.make_async_copy(far, near, in_sem.at[i])
        for i, (far, near) in enumerate(
            (
                (x_hbm, x_ref),
                (cot_hbm, cot_ref),
                (lists_hbm, lists_ref),
                (rule_hbm, rule_ref),
                (w1_hbm, w1_ref),
                (w2_hbm, w2_ref),
            )
        )
    )
    barrier = pltpu.get_barrier_semaphore()
    for fetch in (x_in, cot_in, lists_in, rule_in, w2_in, w1_in):
        fetch.start()
    beside = lax.rem(t + 2 * core - 1 + count, count)
    pl.semaphore_signal(barrier, inc=1, device_id={"tile": peer})
    pl.semaphore_signal(barrier, inc=1, device_id={"tile": beside})
    for d in range(1, chips):
        pl.semaphore_signal(barrier, inc=1, device_id={"tile": there(d)})

    def halo_copy(phase, up):
        return pltpu.make_async_remote_copy(
            src_ref=hsend.at[phase, up],
            dst_ref=halo.at[phase, 1 - up],
            send_sem=hs_sem.at[phase, up],
            recv_sem=hr_sem.at[phase, 1 - up],
            device_id={"tile": t + 2 * up - 1},
        )

    def pick_boundary(phase):
        for up in range(2):
            listed = jnp.broadcast_to(lists_ref[:, up : up + 1], (2 * width, LANES))
            chosen = jnp.zeros((2 * width, LANES), F32)
            for q in range(blocks):
                chosen = jnp.where(listed == q, own[phase, q], chosen)
            hsend[phase, up] = chosen.astype(BF)

    def send_halo(phase):
        @pl.when(t > 0)
        def _():
            halo_copy(phase, 0).start()

        @pl.when(t < count - 1)
        def _():
            halo_copy(phase, 1).start()

    def wait_halo(phase):
        @pl.when(t > 0)
        def _():
            halo_copy(phase, 1).wait_recv()

        @pl.when(t == 0)
        def _():
            halo[phase, 0] = jnp.zeros((2 * width, LANES), BF)

        @pl.when(t < count - 1)
        def _():
            halo_copy(phase, 0).wait_recv()

        @pl.when(t == count - 1)
        def _():
            halo[phase, 1] = jnp.zeros((2 * width, LANES), BF)

    def wait_sent(phase):
        @pl.when(t > 0)
        def _():
            halo_copy(phase, 0).wait_send()

        @pl.when(t < count - 1)
        def _():
            halo_copy(phase, 1).wait_send()

    for fetch in (x_in, cot_in, lists_in):
        fetch.wait()
    for q in range(blocks):
        own[0, q] = jnp.concatenate([x_ref[:, lanes(q)], cot_ref[:, lanes(q)]], axis=0).astype(F32)
    pick_boundary(0)
    pl.semaphore_wait(barrier, chips + 1)
    send_halo(0)

    rule_in.wait()
    reach = jax.lax.broadcasted_iota(jnp.int32, (LANES, LANES), 0)
    firsts = {}
    for a in range(3):
        for b in range(blocks):
            base = b * LANES
            if a != 1:
                low = rule_ref[a * group : a * group + 1, lanes(b)]
                for j in range(1, group):
                    k = a * group + j
                    low = jnp.minimum(low, rule_ref[k : k + 1, lanes(b)])
                low = jnp.min(low, axis=1, keepdims=True)
                firsts[a, b] = low
                base = jnp.zeros_like(low)
                for q in range(1, blocks + 2):
                    base = jnp.where((low >= q * LANES) & (low < missing), q * LANES, base)
            for j in range(group):
                k = a * group + j
                row = rule_ref[k : k + 1, lanes(b)] - base
                hit = jnp.broadcast_to(row, (LANES, LANES)) == reach
                hot[a, b, :, lanes(j)] = jnp.where(hit, 1.0, 0.0).astype(BF)

    w2_in.wait()
    w1_in.wait()
    for w_ref, m_ref in ((w2_ref, mir2), (w1_ref, mir1)):
        for k in range(0, offsets, 2):
            last = min(k + 2, offsets)
            stack = [
                w_ref[:, (offsets - 1 - i) * width : (offsets - i) * width].astype(F32)
                for i in range(k, last)
            ]
            stack = jnp.concatenate(stack, axis=0) if len(stack) > 1 else stack[0]
            m_ref[:, k * width : last * width] = stack.T.astype(BF)

    def gather(phase, a, b):
        if a == 1:
            source = own[phase, b]
        else:
            low = jnp.broadcast_to(firsts[a, b], (2 * width, LANES))
            source = None
            for q in range(blocks):
                if q != b:
                    block = own[phase, q]
                    if source is None:
                        source = block
                    else:
                        source = jnp.where((low >= q * LANES) & (low < (q + 1) * LANES), block, source)
            rim = halo[phase, a // 2].astype(F32)
            source = jnp.where((low >= rows) & (low < missing), rim, source)
        source = source.astype(BF)
        for j in range(0, group, 2):
            last = min(j + 2, group)
            res = jnp.dot(
                source, hot[a, b, :, j * LANES : last * LANES], preferred_element_type=F32
            ).astype(BF)
            for i in range(j, last):
                k = a * group + i
                gat_a[k * width : (k + 1) * width, lanes(b)] = res[:width, lanes(i - j)]
                gat_b[k * width : (k + 1) * width, lanes(b)] = res[width:, lanes(i - j)]

    for b in range(blocks):
        gather(0, 1, b)
    wait_halo(0)
    for a in (0, 2):
        for b in range(blocks):
            gather(0, a, b)

    pre = jnp.dot(w1_ref[...], gat_a[...], preferred_element_type=F32)
    d_hidden = jnp.dot(mir2[...], gat_b[...], preferred_element_type=F32)
    sigma = 1.0 / (1.0 + jnp.exp(-pre))
    hidden = (pre * sigma).astype(BF)
    d_pre = (d_hidden * sigma * (1.0 + pre * (1.0 - sigma))).astype(BF)
    both = jnp.concatenate([hidden, d_pre], axis=0).astype(F32)
    for q in range(blocks):
        own[1, q] = both[:, lanes(q)]
    pick_boundary(1)
    send_halo(1)

    cols = offsets * width
    to_peer = pltpu.make_async_remote_copy(
        src_ref=part.at[1 - core],
        dst_ref=peer_in,
        send_sem=p_sem.at[0],
        recv_sem=p_sem.at[1],
        device_id={"tile": peer},
    )
    spare = part.shape[2] - cols
    if spare:
        for g in range(2):
            part[g, :, cols:] = jnp.zeros((width, spare), F32)
    part[0, :, :cols] = lax.dot_general(d_pre, gat_a[...], TRANS_RHS, preferred_element_type=F32)

    @pl.when(core == 1)
    def _():
        to_peer.start()

    for k in range(0, offsets, 2):
        last = min(k + 2, offsets)
        top = (offsets - k) * width
        terms = lax.dot_general(
            gat_b[(offsets - last) * width : top, :], hidden, TRANS_RHS, preferred_element_type=F32
        )
        pieces = [
            terms[(last - 1 - i) * width : (last - i) * width, :] for i in range(k, last)
        ]
        pieces = jnp.concatenate(pieces, axis=1) if len(pieces) > 1 else pieces[0]
        part[1, :, k * width : last * width] = pieces

    @pl.when(core == 0)
    def _():
        to_peer.start()

    for b in range(blocks):
        gather(1, 1, b)

    def piece(j):
        return piece_of(plan, j)

    to_peer.wait_recv()
    for j in range(chips):
        r, c = piece(j)
        rs_out[j] = (part[core, r, c] + peer_in[r, c]).astype(BF)

    def rs_copy(d):
        target = lax.rem(chip + d, chips)
        return pltpu.make_async_remote_copy(
            src_ref=rs_out.at[target],
            dst_ref=rs_in.at[chip],
            send_sem=rs_s.at[target],
            recv_sem=rs_r.at[chip],
            device_id={"tile": 2 * target + core},
        )

    def rs_arrival(d):
        source = lax.rem(chip + d, chips)
        return source, pltpu.make_async_remote_copy(
            src_ref=rs_out.at[source],
            dst_ref=rs_in.at[source],
            send_sem=rs_s.at[source],
            recv_sem=rs_r.at[source],
            device_id={"tile": 2 * source + core},
        )

    for d in range(1, chips):
        rs_copy(d).start()

    wait_halo(1)
    for a in (0, 2):
        for b in range(blocks):
            gather(1, a, b)
    second = jnp.dot(w2_ref[...], gat_a[...], preferred_element_type=F32)
    out_ref[...] = (second + x_ref[...].astype(F32)).astype(BF)
    d_input = jnp.dot(mir1[...], gat_b[...], preferred_element_type=F32)
    dx_ref[...] = (cot_ref[...].astype(F32) + d_input).astype(BF)
    out_copy = pltpu.make_async_copy(out_ref, out_hbm, done_sem.at[0])
    dx_copy = pltpu.make_async_copy(dx_ref, dx_hbm, done_sem.at[1])
    out_copy.start()
    dx_copy.start()

    total = rs_out[chip].astype(F32)
    for d in range(1, chips):
        source, arrival = rs_arrival(d)
        arrival.wait_recv()
        total = total + rs_in[source].astype(F32)
    mine[...] = (total * scale).astype(BF)
    keep = pltpu.make_async_copy(mine, ag.at[core, chip], done_sem.at[2])

    def ag_copy(d):
        target = lax.rem(chip + d, chips)
        return pltpu.make_async_remote_copy(
            src_ref=mine,
            dst_ref=ag.at[core, chip],
            send_sem=ag_s.at[target],
            recv_sem=ag_r.at[chip],
            device_id={"tile": 2 * target + core},
        )

    def ag_arrival(source):
        return pltpu.make_async_remote_copy(
            src_ref=mine,
            dst_ref=ag.at[core, source],
            send_sem=ag_s.at[source],
            recv_sem=ag_r.at[source],
            device_id={"tile": 2 * source + core},
        )

    def forward(source, held=None):
        return pltpu.make_async_remote_copy(
            src_ref=ag.at[core, source] if held is None else held,
            dst_ref=ag.at[core, source],
            send_sem=fw_s.at[source],
            recv_sem=fw_r.at[source],
            device_id={"tile": peer},
        )

    def forwarded(source):
        return pltpu.make_async_remote_copy(
            src_ref=ag.at[1 - core, source],
            dst_ref=ag.at[1 - core, source],
            send_sem=fw_s.at[source],
            recv_sem=fw_r.at[source],
            device_id={"tile": peer},
        )

    for d in range(1, chips):
        ag_copy(d).start()
    forward(chip, mine).start()
    keep.start()
    for d in range(1, chips):
        source = lax.rem(chip + chips - d, chips)
        ag_arrival(source).wait_recv()
        forward(source).start()
    for j in range(chips):
        forwarded(j).wait_recv()
    wait_sent(0)
    wait_sent(1)
    to_peer.wait_send()
    for d in range(1, chips):
        rs_copy(d).wait_send()
        ag_copy(d).wait_send()
    for j in range(chips):
        forward(j).wait_send()
    for copy in (out_copy, dx_copy, keep):
        copy.wait()


def body(count, features, rulebook, send_lists, weight_first, weight_second, cotangent):
    width, rows = features.shape
    offsets = rulebook.shape[0]
    cols = offsets * width
    blocks = rows // LANES
    chips = count // 2
    plan = chunk_plan(width, cols, chips)
    row_parts, col_parts, piece_rows, piece_cols = plan
    scale = 1.0 / math.sqrt(rows * count)
    dma = pltpu.SemaphoreType.DMA
    hbm = pl.BlockSpec(memory_space=pltpu.HBM)
    results = pl.pallas_call(
        functools.partial(kernel, count, plan, scale),
        out_shape=(
            jax.ShapeDtypeStruct((width, rows), BF),
            jax.ShapeDtypeStruct((width, rows), BF),
            jax.ShapeDtypeStruct((2, chips, piece_rows, piece_cols), BF),
        ),
        in_specs=[hbm] * 6,
        out_specs=(hbm,) * 3,
        scratch_shapes=[
            pltpu.VMEM((width, rows), BF),
            pltpu.VMEM((width, rows), BF),
            pltpu.VMEM((piece_rows, piece_cols), BF),
            dma((3,)),
            pltpu.VMEM((width, rows), BF),
            pltpu.VMEM((offsets, rows), jnp.int32),
            pltpu.VMEM((1, 2), jnp.int32),
            pltpu.VMEM((width, cols), BF),
            pltpu.VMEM((width, cols), BF),
            pltpu.VMEM((width, rows), BF),
            dma((6,)),
            pltpu.VMEM((3, blocks, LANES, offsets // 3 * LANES), BF),
            pltpu.VMEM((cols, rows), BF),
            pltpu.VMEM((cols, rows), BF),
            pltpu.VMEM((width, cols), BF),
            pltpu.VMEM((width, cols), BF),
            pltpu.VMEM((2, blocks, 2 * width, LANES), F32),
            pltpu.VMEM((2, 2, 2 * width, LANES), BF),
            pltpu.VMEM((2, 2, 2 * width, LANES), BF),
            pltpu.VMEM((2, width, col_parts * piece_cols), F32),
            pltpu.VMEM((width, col_parts * piece_cols), F32),
            pltpu.VMEM((chips, piece_rows, piece_cols), BF),
            pltpu.VMEM((chips, piece_rows, piece_cols), BF),
            dma((2, 2)),
            dma((2, 2)),
            dma((2,)),
            dma((chips,)),
            dma((chips,)),
            dma((chips,)),
            dma((chips,)),
            dma((chips,)),
            dma((chips,)),
        ],
        compiler_params=pltpu.CompilerParams(
            collective_id=0, has_side_effects=True, vmem_limit_bytes=LIMIT_MIB * 1024 * 1024
        ),
    )(features, rulebook, send_lists.T, weight_first, weight_second, cotangent)
    return pl.pallas_call(
        functools.partial(finish, plan),
        out_shape=(
            jax.ShapeDtypeStruct((width, rows), BF),
            jax.ShapeDtypeStruct((width, rows), BF),
            jax.ShapeDtypeStruct((width, cols), F32),
            jax.ShapeDtypeStruct((width, cols), F32),
        ),
        in_specs=[hbm] * 3,
        out_specs=(hbm,) * 4,
        scratch_shapes=[
            pltpu.VMEM((2, chips, piece_rows, piece_cols), BF),
            pltpu.VMEM((2, width, cols), F32),
            dma((6,)),
        ],
        compiler_params=pltpu.CompilerParams(vmem_limit_bytes=LIMIT_MIB * 1024 * 1024),
    )(*results)


def solution(mesh):
    split = P(None, ("groups", "tile"))
    return jax.shard_map(
        functools.partial(body, mesh.shape["tile"]),
        mesh=mesh,
        in_specs=(split, split, split, P(), P(), split),
        out_specs=(split, split, P("groups", None), P("groups", None)),
        check_vma=False,
    )
```
